128 devices in a mesh: row: 16 (over z_hi, y, core), col: 8 (over x, z_lo).
Axes of the slice: x: 4, y: 4, z: 4 (z_hi: 2, z_lo: 2; z = z_hi * 2 + z_lo), core: 2. Of those that a mesh axis runs over, the one named last changes fastest.
Arguments:
- matrix: bfloat16 [8192, 8192], P('row'), as said below
- position: int32 [128], replicated, may hold values from 0 to 127, as said below
- square_pattern: int32 [128, 128], replicated, may hold values from 0 to 1, as said below
- iterate_pattern: int32 [128, 128], replicated, may hold values from 0 to 1, as said below
Outputs:
- square: bfloat16 [8192, 8192], P('row', 'col')
- iterate: bfloat16 [8192, 8192], P('row', 'col')
The draws below stay inside these ranges and needn't reach their ends.
Inputs may be any that keep to these rules, and one draw needn't show every extreme that they name: matrix is exactly symmetric. A permutation; the 8 blocks b that share b // 8 have distinct values of position // 8. `square_pattern`: symmetric, ones on the diagonal. `iterate_pattern`: symmetric, ones on the diagonal.
All inputs are finite; a program needn't handle non-finite values.
Results may differ from the reference program's by a relative error of at most 0.0043.
Values may be sent and summed in bfloat16 or wider, within the bound.
A program may use at most 128 MiB of HBM per device.

```python
import math
import jax
import jax.numpy as jnp

BW = 64
RB = 8
NB = 128
M = 8192


def draw_matrix(key, part):
    key = jax.random.fold_in(key, 11)
    key_strong, key_noise, key_sign, key_diag = jax.random.split(key, 4)
    picks = jax.random.randint(key_strong, (NB, NB), 0, NB)
    block_eye = jnp.arange(NB)[:, None] == jnp.arange(NB)[None, :]
    strong = ((picks + picks.T) % NB < 4) | block_eye
    block_scale = jnp.where(strong, 1.0, 0.08).astype(jnp.float32)
    amplitude = 0.6 / math.sqrt(BW * (4.0 + 0.0064 * NB))
    noise = jax.random.normal(key_noise, (M, M), jnp.float32)
    symmetric = (noise + noise.T) * 0.70710678
    scale_full = jnp.broadcast_to(block_scale[:, None, :, None], (NB, BW, NB, BW)).reshape(M, M)
    off_diagonal = symmetric * scale_full * amplitude
    signs = jnp.where(jax.random.randint(key_sign, (M,), 0, 2) == 0, -1.0, 1.0).astype(jnp.float32)
    magnitudes = jax.random.uniform(key_diag, (M,), jnp.float32, 0.4, 0.9)
    element_eye = jnp.arange(M)[:, None] == jnp.arange(M)[None, :]
    return jnp.where(element_eye, (signs * magnitudes)[:, None], off_diagonal).astype(jnp.bfloat16)


def pattern_common(key, salt):
    key = jax.random.fold_in(key, salt)
    picks = jax.random.randint(key, (NB, NB), 0, 10)
    totals = picks + picks.T
    block_eye = jnp.arange(NB)[:, None] == jnp.arange(NB)[None, :]
    return jnp.where(block_eye | (totals >= 5), 1, 0).astype(jnp.int32)


def draw_square_pattern(key, part):
    return pattern_common(key, 21)


def draw_iterate_pattern(key, part):
    return pattern_common(key, 22)


def draw_position(key, part):
    key = jax.random.fold_in(key, 7)
    grid_rows = NB // RB
    key_outer, key_shift, key_inner, key_place = jax.random.split(key, 4)
    outer = jax.random.permutation(key_outer, grid_rows)
    shifted = jax.random.permutation(key_shift, grid_rows)
    inner = jax.vmap(lambda k: jax.random.permutation(k, RB))(jax.random.split(key_inner, grid_rows))
    placed = jax.vmap(lambda k: jax.random.permutation(k, RB))(jax.random.split(key_place, grid_rows))
    blocks = jnp.arange(NB, dtype=jnp.int32)
    source = blocks // RB
    within = blocks % RB
    slot_number = inner[source, within]
    target = outer[(shifted[source] + slot_number) % grid_rows]
    return (target * RB + placed[target, slot_number]).astype(jnp.int32)


def setup_inputs(seed: int = 0) -> dict:
    arg_keys = jax.random.split(jax.random.key(seed), 5)
    return {
        "matrix": draw_matrix(jax.random.fold_in(arg_keys[4], 71), 0),
        "position": draw_position(jax.random.fold_in(arg_keys[4], 71), 0),
        "square_pattern": draw_square_pattern(jax.random.fold_in(arg_keys[4], 71), 0),
        "iterate_pattern": draw_iterate_pattern(jax.random.fold_in(arg_keys[4], 71), 0),
    }


def to_grid(values, inverse):
    blocks4 = values.reshape(NB, BW, NB, BW)
    blocks4 = jnp.take(blocks4, inverse, axis=0)
    blocks4 = jnp.take(blocks4, inverse, axis=2)
    return blocks4.reshape(M, M)


def filtered(values, pattern):
    blocks4 = values.reshape(NB, BW, NB, BW) * pattern.astype(jnp.float32)[:, None, :, None]
    return blocks4.reshape(M, M)


def reference(matrix, position, square_pattern, iterate_pattern):
    numbers = jnp.arange(NB, dtype=jnp.int32)
    inverse = jnp.sum(jnp.where(position[:, None] == numbers[None, :], numbers[:, None], 0), axis=0).astype(jnp.int32)
    first = jnp.dot(matrix, matrix, preferred_element_type=jnp.float32)
    filtered_square = filtered(first, square_pattern).astype(jnp.bfloat16)
    second = jnp.dot(matrix, filtered_square, preferred_element_type=jnp.float32)
    next_atoms = filtered(0.5 * (3.0 * matrix.astype(jnp.float32) - second), iterate_pattern).astype(jnp.bfloat16)
    return to_grid(filtered_square, inverse), to_grid(next_atoms, inverse)
```

```python
import functools

import jax
import jax.numpy as jnp
from jax import lax
from jax.experimental import pallas as pl
from jax.experimental.pallas import tpu as pltpu
from jax.sharding import PartitionSpec as P

BW = 64
M = 8192
NB = M // BW
ROWS = 512
NR = 16
NC = 8
NCH = 4
CB = NR // NCH
CW = CB * BW
KT = NC * CW
SUB = 16
UNITS = ROWS // SUB
PARTS = ((0, 11), (11, 11), (22, 10))
MESH = pl.DeviceIdType.MESH
BF = jnp.bfloat16
F32 = jnp.float32


def flip(v, b):
    return v + b - 2 * v * b


def kernel(
    first, pair, source, slot, m_hbm, pos_row, sq_pat, it_pat,
    sq_ref, it_ref,
    mine, mg, fg, facc, slots_out, mgp, acc, tt, got1, got2, msq, mit, odd,
    xs, xr, ds, dr, as_, ar, ns, nr, t1s, t1r, t2s, t2r, loc, m_sem, *slots_in,
):
    r = lax.axis_index("row")
    c = lax.axis_index("col")
    k = r % 2
    y = (r // 2) % 4
    zh = r // 8
    x = c // 2
    zl = c % 2
    jz = flip(zl, zh)
    lab = x * 2 + jz

    def row_of(zh_, y_, k_):
        return (zh_ * 4 + y_) * 2 + k_

    def group_col(row):
        return x * 2 + flip(jz, row // 8)

    def outer(mask):
        y_ = y
        if mask & 1:
            y_ = y_ + 1 - 2 * (y_ % 2)
        if mask & 2:
            y_ = 3 - y_
        zh_ = 1 - zh if mask & 4 else zh
        return row_of(zh_, y_, k)

    def inner(mask):
        x_ = x
        if mask & 1:
            x_ = x_ + 1 - 2 * (x_ % 2)
        if mask & 2:
            x_ = 3 - x_
        zl_ = 1 - zl if mask & 4 else zl
        return x_, zl_

    def inner_lab(mask):
        x_, zl_ = inner(mask)
        return x_ * 2 + flip(zl_, zh)

    outer_dev = [(outer(1 << d), group_col(outer(1 << d))) for d in range(3)]
    inner_dev = [(r, inner(1 << d)[0] * 2 + inner(1 << d)[1]) for d in range(3)]
    sibling = (r + 1 - 2 * k, c)

    @pl.loop(0, NB // 2)
    def _(i):
        at = pl.ds(pl.multiple_of(i * 128, 128), 128)
        pltpu.make_async_copy(m_hbm.at[:, at], mine.at[i], m_sem).start()

    barrier = pltpu.get_barrier_semaphore()
    for d in range(1, NR):
        t = lax.rem(r + d, NR)
        pl.semaphore_signal(barrier, inc=1, device_id=(t, group_col(t)), device_id_type=MESH)
    for d in range(1, NC):
        pl.semaphore_signal(
            barrier, inc=1, device_id=(r, lax.rem(c + d, NC)), device_id_type=MESH
        )

    block_id = lax.broadcasted_iota(jnp.int32, (NR, NB), 0)
    cols_hot = (pos_row[...] == 8 * block_id + lab).astype(F32)
    row_id = lax.broadcasted_iota(jnp.int32, (8, NB), 0)
    rows_hot = (pos_row[...] == 8 * r + row_id).astype(F32)
    wide = (
        lax.broadcasted_iota(jnp.int32, (NR, NR * BW), 1) // BW
        == lax.broadcasted_iota(jnp.int32, (NR, NR * BW), 0)
    ).astype(F32)

    def columns_of(rows):
        small = lax.dot_general(
            rows, cols_hot, (((1,), (1,)), ((), ())), preferred_element_type=F32
        )
        return jnp.dot(small, wide, preferred_element_type=F32)

    parity = (lax.broadcasted_iota(jnp.int32, (8, NB), 1) % 2).astype(F32)
    odd[...] = columns_of(parity)
    msq[...] = columns_of(sq_pat[pl.ds(pl.multiple_of(8 * r, 8), 8), :].astype(F32))
    mit[...] = columns_of(
        jnp.dot(rows_hot, it_pat[...].astype(F32), preferred_element_type=F32)
    )

    lane = lax.broadcasted_iota(jnp.int32, (ROWS, 2 * BW), 1)
    pltpu.make_async_copy(mine, mine, m_sem).wait()
    for i in range(NR // 2):
        w0 = mine[pair[8 * (2 * i) + lab]].astype(F32)
        w1 = mine[pair[8 * (2 * i + 1) + lab]].astype(F32)
        o = odd[0:1, i * 128 : (i + 1) * 128]
        lo = w0 * (1.0 - o) + pltpu.roll(w0, BW, 1) * o
        hi = w1 * o + pltpu.roll(w1, BW, 1) * (1.0 - o)
        both = jnp.where(lane < BW, lo, hi).astype(BF).reshape(UNITS, SUB, 128)
        j, off = (2 * i) // CB, ((2 * i) % CB) * BW
        mg[j, pl.ds(r * UNITS, UNITS), :, off : off + 128] = both

    pl.semaphore_wait(barrier, NR + NC - 2)

    def subs(order, o):
        out = [0]
        for d in order[:o]:
            out += [s | (1 << d) for s in out]
        return out

    def outer_copy(j, p, sub, d):
        lo, n = PARTS[p]
        at = mg.at[j, pl.ds(outer(sub) * UNITS + lo, n)]
        mask = sub | (1 << d)
        return pltpu.make_async_remote_copy(
            src_ref=at, dst_ref=at, send_sem=xs.at[j, p, mask - 1], recv_sem=xr.at[j, p, mask - 1],
            device_id=outer_dev[d], device_id_type=MESH,
        )

    def outer_arrival(j, p, mask, d):
        lo, n = PARTS[p]
        at = mg.at[j, pl.ds(outer(mask) * UNITS + lo, n)]
        return pltpu.make_async_remote_copy(
            src_ref=at, dst_ref=at, send_sem=xs.at[j, p, mask - 1], recv_sem=xr.at[j, p, mask - 1],
            device_id=outer_dev[d], device_id_type=MESH,
        )

    def inner_copy(j, p, sub, d, m):
        lo, n = PARTS[p]
        at = fg.at[j, pl.ds(lo * SUB, n * SUB), pl.ds(pl.multiple_of(inner_lab(sub) * CW, CW), CW)]
        return pltpu.make_async_remote_copy(
            src_ref=at, dst_ref=at, send_sem=ns.at[j, p, m - 1], recv_sem=nr.at[j, p, m - 1],
            device_id=inner_dev[d], device_id_type=MESH,
        )

    def orders():
        for p in range(3):
            yield p, [(p + i) % 3 for i in range(3)]

    def outer_send(j, o):
        for sub_i in range(1 << o):
            for p, order in orders():
                outer_copy(j, p, subs(order, o)[sub_i], order[o]).start()

    def outer_wait(j, o):
        for p, order in orders():
            for sub in subs(order, o):
                outer_arrival(j, p, sub | (1 << order[o]), order[o]).wait_recv()

    def inner_send(j, o):
        for sub_i in range(1 << o):
            for p, order in orders():
                sub = subs(order, o)[sub_i]
                inner_copy(j, p, sub, order[o], sub | (1 << order[o])).start()

    def inner_wait(j, o):
        for p, order in orders():
            for sub in subs(order, o):
                m = sub | (1 << order[o])
                inner_copy(j, p, m, order[o], m).wait_recv()

    def sib_copy(j, m, mine=True):
        row = outer(m)
        if not mine:
            row = row + 1 - 2 * k
        at = mg.at[j, pl.ds(row * UNITS, UNITS)]
        return pltpu.make_async_remote_copy(
            src_ref=at, dst_ref=at, send_sem=ds.at[j, m], recv_sem=dr.at[j, m],
            device_id=sibling, device_id_type=MESH,
        )

    def a2a_copy(j, t, src_row):
        return pltpu.make_async_remote_copy(
            src_ref=slots_out.at[j, t], dst_ref=slots_in[j].at[src_row],
            send_sem=as_.at[j, t], recv_sem=ar.at[j, src_row],
            device_id=(t, group_col(t)), device_id_type=MESH,
        )

    def a2a_local(j):
        return pltpu.make_async_copy(slots_out.at[j, r], slots_in[j].at[r], loc.at[j])

    def first_product(j):
        facc[...] = jnp.zeros_like(facc)

        @pl.loop(0, 8)
        def _(kt):
            left = jnp.concatenate([mine[kt * 8 + i] for i in range(8)], axis=1)
            right = mg[j, pl.ds(kt * 64, 64)].reshape(1024, CW)
            prod = jnp.dot(left, right, preferred_element_type=F32)
            facc[...] += prod.reshape(8, BW, CW)

        for a in range(8):
            facc[a] = facc[a] * msq[a : a + 1, j * CW : (j + 1) * CW]
        for t in range(NR):
            slots_out[j, t] = facc[slot[NR * r + t]].astype(BF)

    def a2a_send(j):
        for d in range(1, NR):
            a2a_copy(j, lax.rem(r + d, NR), r).start()
        a2a_local(j).start()

    def a2a_wait(j):
        for d in range(1, NR):
            t = lax.rem(r + NR - d, NR)
            a2a_copy(j, t, t).wait_recv()
        a2a_local(j).wait()

    def take_rows(j):
        for p in range(8):
            fg[j, p * BW : (p + 1) * BW, pl.ds(pl.multiple_of(lab * CW, CW), CW)] = slots_in[j][
                source[8 * r + p]
            ]

    def second_product(j):
        @pl.loop(0, NC)
        def _(n):
            for i in range(CB):
                src = first[8 * (j * CB + i) + n]
                for u in range(BW // SUB):
                    at = pl.ds(pl.multiple_of(n * CW + i * BW + u * SUB, SUB), SUB)
                    for jj in range(NCH):
                        mgp[at, jj * CW : (jj + 1) * CW] = mg[jj, src + u]

        @pl.loop(0, M // NC // 256)
        def _(nt):
            at = pl.ds(pl.multiple_of(nt * 256, 256), 256)
            prod = jnp.dot(fg[j], mgp[:, at], preferred_element_type=F32)
            if j == 0:
                acc[:, at] = prod
            else:
                acc[:, at] += prod

    def last_piece(jj):
        for p in range(8):
            src = first[8 * r + p]
            for u in range(BW // SUB):
                own = mg[jj, src + u].astype(F32)
                lo = p * BW + u * SUB
                at = (slice(lo, lo + SUB), slice(jj * CW, (jj + 1) * CW))
                acc[at] = (0.5 * (3.0 * own - acc[at])) * mit[p : p + 1, jj * CW : (jj + 1) * CW]
        turned = acc[:, jj * CW : (jj + 1) * CW].T.astype(BF)
        for i in range(CB):
            tt[jj * CB + i] = turned[i * BW : (i + 1) * BW, :]

    def turn1(t, src_row):
        return pltpu.make_async_remote_copy(
            src_ref=tt.at[t], dst_ref=got1.at[src_row], send_sem=t1s.at[t], recv_sem=t1r.at[src_row],
            device_id=(t, group_col(t)), device_id_type=MESH,
        )

    def turn2(col, src_lab):
        return pltpu.make_async_remote_copy(
            src_ref=got1.at[pl.ds(2 * col, 2)], dst_ref=got2.at[src_lab],
            send_sem=t2s.at[col], recv_sem=t2r.at[src_lab],
            device_id=(r, col), device_id_type=MESH,
        )

    def square_out():
        jc = c // (NC // NCH)
        i0 = (2 * c) % CB
        for h in range(4):
            w = [
                fg[jc, :, pl.ds(pl.multiple_of(n * CW + i0 * BW, 128), 128)].astype(F32)
                for n in (2 * h, 2 * h + 1)
            ]
            sq_ref[:, h * 128 : (h + 1) * 128] = jnp.where(
                lane < BW, w[0], pltpu.roll(w[1], BW, 1)
            ).astype(BF)
            sq_ref[:, 512 + h * 128 : 512 + (h + 1) * 128] = jnp.where(
                lane < BW, pltpu.roll(w[0], BW, 1), w[1]
            ).astype(BF)

    def when(j, f, *args):
        if 0 <= j < NCH:
            f(j, *args)

    for i in range(NCH + 8):
        when(i, outer_send, 0)
        if 0 <= i - 1 < NCH:
            outer_wait(i - 1, 0)
            outer_send(i - 1, 1)
        if 0 <= i - 2 < NCH:
            outer_wait(i - 2, 1)
            outer_send(i - 2, 2)
        if 0 <= i - 3 < NCH:
            outer_wait(i - 3, 2)
            for m in range(8):
                sib_copy(i - 3, m).start()
        if 0 <= i - 5 < NCH:
            a2a_wait(i - 5)
            take_rows(i - 5)
            inner_send(i - 5, 0)
        if 0 <= i - 6 < NCH:
            inner_wait(i - 6, 0)
            inner_send(i - 6, 1)
        if 0 <= i - 7 < NCH:
            inner_wait(i - 7, 1)
            inner_send(i - 7, 2)
        if 0 <= i - 4 < NCH:
            for m in range(8):
                sib_copy(i - 4, m, mine=False).wait_recv()
            first_product(i - 4)
            a2a_send(i - 4)
        if 0 <= i - 8 < NCH:
            inner_wait(i - 8, 2)
            second_product(i - 8)

    for jj in range(NCH):
        last_piece(jj)
        for i in range(CB):
            t = jj * CB + i

            @pl.when(t != r)
            def _():
                turn1(t, r).start()

            @pl.when(t == r)
            def _():
                pltpu.make_async_copy(tt.at[t], got1.at[t], loc.at[NCH]).start()

    square_out()
    for d in range(1, NR):
        t = lax.rem(r + NR - d, NR)
        turn1(t, t).wait_recv()
    pltpu.make_async_copy(tt.at[r], got1.at[r], loc.at[NCH]).wait()
    for d in range(1, NC):
        turn2(lax.rem(c + d, NC), lab).start()
    here = pltpu.make_async_copy(got1.at[pl.ds(2 * c, 2)], got2.at[lab], loc.at[NCH + 1])
    here.start()
    for n in range(1, NC):
        col = lax.rem(c + NC - n, NC)
        src = 2 * (col // 2) + flip(col % 2, zh)
        turn2(col, src).wait_recv()
    here.wait()
    for n in range(NC):
        for h in range(2):
            it_ref[n * BW : (n + 1) * BW, h * ROWS : (h + 1) * ROWS] = got2[n, h]

    for j in range(NCH):
        for o in range(3):
            for p, order in orders():
                for sub in subs(order, o):
                    outer_copy(j, p, sub, order[o]).wait_send()
                    inner_copy(j, p, sub, order[o], sub | (1 << order[o])).wait_send()
        for m in range(8):
            sib_copy(j, m).wait_send()
        for d in range(1, NR):
            a2a_copy(j, lax.rem(r + d, NR), r).wait_send()
    for d in range(1, NR):
        turn1(lax.rem(r + d, NR), r).wait_send()
    for d in range(1, NC):
        turn2(lax.rem(c + d, NC), lab).wait_send()


def per_device(matrix, position, square_pattern, iterate_pattern):
    numbers = jnp.arange(NB, dtype=jnp.int32)
    inverse = jnp.sum(jnp.where(position[:, None] == numbers[None, :], numbers[:, None], 0), axis=0)
    target = position.reshape(NR, 1, 8) // 8
    hits = target == jnp.arange(NR, dtype=jnp.int32)[None, :, None]
    slot = jnp.sum(jnp.where(hits, jnp.arange(8, dtype=jnp.int32), 0), axis=2)
    vmem = pl.BlockSpec(memory_space=pltpu.VMEM)
    smem = pl.BlockSpec(memory_space=pltpu.SMEM)
    dma = pltpu.SemaphoreType.DMA
    return pl.pallas_call(
        kernel,
        out_shape=[jax.ShapeDtypeStruct((ROWS, M // NC), BF)] * 2,
        in_specs=[smem] * 4 + [pl.BlockSpec(memory_space=pl.ANY), vmem, vmem, vmem],
        out_specs=[vmem, vmem],
        scratch_shapes=[
            pltpu.VMEM((NB // 2, ROWS, 2 * BW), BF),
            pltpu.VMEM((NCH, M // SUB, SUB, CW), BF),
            pltpu.VMEM((NCH, ROWS, KT), BF),
            pltpu.VMEM((8, BW, CW), F32),
            pltpu.VMEM((NCH, NR, BW, CW), BF),
            pltpu.VMEM((KT, M // NC), BF),
            pltpu.VMEM((ROWS, M // NC), F32),
            pltpu.VMEM((NR, BW, ROWS), BF),
            pltpu.VMEM((NR, BW, ROWS), BF),
            pltpu.VMEM((NC, 2, BW, ROWS), BF),
            pltpu.VMEM((8, M // NC), F32),
            pltpu.VMEM((8, M // NC), F32),
            pltpu.VMEM((8, M // NC), F32),
            dma((NCH, 3, 7)), dma((NCH, 3, 7)),
            dma((NCH, 8)), dma((NCH, 8)),
            dma((NCH, NR)), dma((NCH, NR)),
            dma((NCH, 3, 7)), dma((NCH, 3, 7)),
            dma((NR,)), dma((NR,)),
            dma((NC,)), dma((NC,)),
            dma((NCH + 2,)),
            dma,
            *[pltpu.VMEM((NR, BW, CW), BF)] * NCH,
        ],
        compiler_params=pltpu.CompilerParams(
            collective_id=0, has_side_effects=True, vmem_limit_bytes=60 << 20
        ),
        cost_estimate=pl.CostEstimate(
            flops=4 * ROWS * M * (M // NC), bytes_accessed=12 << 20, transcendentals=0
        ),
        name="sign_step",
    )(
        inverse * (BW // SUB), inverse // 2, inverse // 8, slot.reshape(-1),
        matrix, position.reshape(1, NB),
        square_pattern, iterate_pattern,
    )


def solution(mesh):
    return jax.shard_map(
        per_device,
        mesh=mesh,
        in_specs=(P("row", None), P(), P(), P()),
        out_specs=(P("row", "col"), P("row", "col")),
        check_vma=False,
    )
```

```python
import jax
import jax.numpy as jnp
from jax import lax
from jax.experimental import pallas as pl
from jax.experimental.pallas import tpu as pltpu
from jax.sharding import PartitionSpec as P

BW = 64
M = 8192
NB = M // BW
ROWS = 512
NR = 16
NC = 8
COLS = M // NC
NCH = 4
CB = NR // NCH
CW = CB * BW
KT = NC * CW
SUB = 16
UNITS = ROWS // SUB
PARTS = ((0, 11), (11, 11), (22, 10))
U = 4
UR = BW // U
MESH = pl.DeviceIdType.MESH
BF = jnp.bfloat16
F32 = jnp.float32


def flip(v, b):
    return v + b - 2 * v * b


def subs(order, o):
    out = [0]
    for d in order[:o]:
        out += [s | (1 << d) for s in out]
    return out


def stage(o):
    for i in range(1 << o):
        for p in range(3):
            order = [(p + n) % 3 for n in range(3)]
            yield p, subs(order, o)[i], order[o]


def kernel(
    first, pair, m_hbm, pos_row, sq_pat, it_pat,
    sq_ref, it_ref,
    mine, mg, fg, facc, mgp, acc, turned, spread, msq, mit, odd, odd_all,
    xs, xr, ds, dr, ns, nr, t1s, t1r, t2s, t2r, loc, m_sem, *got,
):
    r = lax.axis_index("row")
    c = lax.axis_index("col")
    k = r % 2
    y = (r // 2) % 4
    zh = r // 8
    x = c // 2
    zl = c % 2
    jz = flip(zl, zh)
    lab = x * 2 + jz

    def group_col(row):
        return x * 2 + flip(jz, row // 8)

    def outer(mask):
        y_ = y
        if mask & 1:
            y_ = y_ + 1 - 2 * (y_ % 2)
        if mask & 2:
            y_ = 3 - y_
        zh_ = 1 - zh if mask & 4 else zh
        return (zh_ * 4 + y_) * 2 + k

    def inner(mask):
        x_ = x
        if mask & 1:
            x_ = x_ + 1 - 2 * (x_ % 2)
        if mask & 2:
            x_ = 3 - x_
        zl_ = 1 - zl if mask & 4 else zl
        return x_ * 2 + zl_

    def label(col):
        return col // 2 * 2 + flip(col % 2, zh)

    outer_dev = [(outer(1 << d), group_col(outer(1 << d))) for d in range(3)]
    inner_dev = [(r, inner(1 << d)) for d in range(3)]
    sibling = (r + 1 - 2 * k, c)

    def outer_copy(j, p, mask, d, held):
        lo, n = PARTS[p]
        at = mg.at[j, pl.ds(outer(held) * UNITS + lo, n)]
        return pltpu.make_async_remote_copy(
            src_ref=at, dst_ref=at, send_sem=xs.at[j, p, mask - 1], recv_sem=xr.at[j, p, mask - 1],
            device_id=outer_dev[d], device_id_type=MESH,
        )

    def inner_copy(j, p, mask, d, held):
        lo, n = PARTS[p]
        at = fg.at[
            j, pl.ds(lo * SUB, n * SUB), pl.ds(pl.multiple_of(label(inner(held)) * CW, CW), CW)
        ]
        return pltpu.make_async_remote_copy(
            src_ref=at, dst_ref=at, send_sem=ns.at[j, p, mask - 1], recv_sem=nr.at[j, p, mask - 1],
            device_id=inner_dev[d], device_id_type=MESH,
        )

    def sib_copy(j, p, mask, theirs=False):
        lo, n = PARTS[p]
        row = outer(mask)
        if theirs:
            row = row + 1 - 2 * k
        at = mg.at[j, pl.ds(row * UNITS + lo, n)]
        return pltpu.make_async_remote_copy(
            src_ref=at, dst_ref=at, send_sem=ds.at[j, p, mask], recv_sem=dr.at[j, p, mask],
            device_id=sibling, device_id_type=MESH,
        )

    def outer_send(j, o):
        for p, sub, d in stage(o):
            outer_copy(j, p, sub | (1 << d), d, sub).start()

    def outer_wait(j, o):
        for p, sub, d in stage(o):
            mask = sub | (1 << d)
            outer_copy(j, p, mask, d, mask).wait_recv()
            sib_copy(j, p, mask).start()

    def inner_send(j, o):
        for p, sub, d in stage(o):
            inner_copy(j, p, sub | (1 << d), d, sub).start()

    def inner_wait(j, o):
        for p, sub, d in stage(o):
            mask = sub | (1 << d)
            inner_copy(j, p, mask, d, mask).wait_recv()

    def sib_wait(j):
        for mask in range(8):
            for p in range(3):
                sib_copy(j, p, mask, theirs=True).wait_recv()

    def turn1(w, u, t, src_row):
        return pltpu.make_async_remote_copy(
            src_ref=turned.at[w, u, t], dst_ref=got[w * U + u].at[pl.ds(4 * src_row, 4)],
            send_sem=t1s.at[w, u, t], recv_sem=t1r.at[w, u, src_row],
            device_id=(t, group_col(t)), device_id_type=MESH,
        )

    def turn1_own(w, u):
        return pltpu.make_async_copy(
            turned.at[w, u, r], got[w * U + u].at[pl.ds(4 * r, 4)], loc.at[0, w, u]
        )

    def turn2(w, u, col, src_lab):
        out = (sq_ref, it_ref)[w]
        return pltpu.make_async_remote_copy(
            src_ref=spread.at[w, u, col],
            dst_ref=out.at[pl.ds(pl.multiple_of(src_lab * BW + u * UR, UR), UR)],
            send_sem=t2s.at[w, u, col], recv_sem=t2r.at[w, u, src_lab],
            device_id=(r, col), device_id_type=MESH,
        )

    def turn2_own(w, u):
        out = (sq_ref, it_ref)[w]
        return pltpu.make_async_copy(
            spread.at[w, u, c],
            out.at[pl.ds(pl.multiple_of(lab * BW + u * UR, UR), UR)],
            loc.at[1, w, u],
        )

    def turn_store(w, j, values):
        flat = values.T.astype(BF)
        for i in range(CB):
            for u in range(U):
                for n in range(4):
                    lo = i * BW + u * UR
                    turned[w, u, j * CB + i, n] = flat[lo : lo + UR, n * 128 : (n + 1) * 128]

    def turn1_send(w, u):
        for d in range(1, NR):
            turn1(w, u, lax.rem(r + d, NR), r).start()
        turn1_own(w, u).start()

    def turn_on(w, u):
        for d in range(1, NR):
            t = lax.rem(r + NR - d, NR)
            turn1(w, u, t, t).wait_recv()
        turn1_own(w, u).wait()
        have = got[w * U + u]
        lane = lax.broadcasted_iota(jnp.int32, (UR, 128), 1)
        for col in range(NC):
            for g in range(8):
                q = 16 * col + 2 * g
                w0 = have[pair[q]].astype(F32)
                w1 = have[pair[q + 1]].astype(F32)
                o = odd_all[q // 2 : q // 2 + 1, :]
                lo = w0 * (1.0 - o) + pltpu.roll(w0, BW, 1) * o
                hi = w1 * o + pltpu.roll(w1, BW, 1) * (1.0 - o)
                spread[w, u, col, :, g * 128 : (g + 1) * 128] = jnp.where(
                    lane < BW, lo, hi
                ).astype(BF)
        for d in range(1, NC):
            turn2(w, u, lax.rem(c + d, NC), lab).start()
        turn2_own(w, u).start()

    def turn_end(w, u):
        for d in range(1, NC):
            col = lax.rem(c + NC - d, NC)
            turn2(w, u, col, label(col)).wait_recv()
        turn2_own(w, u).wait()

    def columns(j):
        lane = lax.broadcasted_iota(jnp.int32, (ROWS, 2 * BW), 1)
        for i in range(j * CB // 2, (j + 1) * CB // 2):
            w0 = mine[pair[8 * (2 * i) + lab]].astype(F32)
            w1 = mine[pair[8 * (2 * i + 1) + lab]].astype(F32)
            o = odd[0:1, i * 128 : (i + 1) * 128]
            lo = w0 * (1.0 - o) + pltpu.roll(w0, BW, 1) * o
            hi = w1 * o + pltpu.roll(w1, BW, 1) * (1.0 - o)
            both = jnp.where(lane < BW, lo, hi).astype(BF).reshape(UNITS, SUB, 128)
            off = (2 * i) % CB * BW
            mg[j, pl.ds(r * UNITS, UNITS), :, off : off + 128] = both

    def columns_of(rows):
        block_id = lax.broadcasted_iota(jnp.int32, (NR, NB), 0)
        hot = (pos_row[...] == 8 * block_id + lab).astype(F32)
        wide = (
            lax.broadcasted_iota(jnp.int32, (NR, COLS), 1) // BW
            == lax.broadcasted_iota(jnp.int32, (NR, COLS), 0)
        ).astype(F32)
        small = lax.dot_general(rows, hot, (((1,), (1,)), ((), ())), preferred_element_type=F32)
        return jnp.dot(small, wide, preferred_element_type=F32)

    def filters():
        at = pl.ds(pl.multiple_of(8 * r, 8), 8)
        msq[...] = columns_of(sq_pat[at, :].astype(F32))
        mit[...] = columns_of(it_pat[at, :].astype(F32))
        parity = (lax.broadcasted_iota(jnp.int32, (NB, NB), 0) % 2).astype(F32)
        half = lax.broadcasted_iota(jnp.int32, (NB // 2, NB), 0)
        evens = (pos_row[...] == 2 * half).astype(F32)
        odds = (pos_row[...] == 2 * half + 1).astype(F32)
        lane = lax.broadcasted_iota(jnp.int32, (NB // 2, NB), 1)
        odd_all[...] = jnp.where(
            lane < BW,
            jnp.dot(evens, parity, preferred_element_type=F32),
            jnp.dot(odds, parity, preferred_element_type=F32),
        )

    def first_product(j):
        facc[...] = jnp.zeros_like(facc)

        @pl.loop(0, 8)
        def _(kt):
            left = jnp.concatenate([mine[kt * 8 + i] for i in range(8)], axis=1)
            right = mg[j, pl.ds(kt * 64, 64)].reshape(1024, CW)
            facc[...] += jnp.dot(left, right, preferred_element_type=F32)

        at = pl.ds(pl.multiple_of(lab * CW, CW), CW)
        for a in range(8):
            rows = slice(a * BW, (a + 1) * BW)
            value = facc[rows, :] * msq[a : a + 1, j * CW : (j + 1) * CW]
            facc[rows, :] = value
            fg[j, rows, at] = value.astype(BF)

    def second_product(j):
        @pl.loop(0, NC)
        def _(n):
            for i in range(CB):
                src = first[8 * (j * CB + i) + n]
                for u in range(BW // SUB):
                    at = pl.ds(pl.multiple_of(n * CW + i * BW + u * SUB, SUB), SUB)
                    for jj in range(NCH):
                        mgp[at, jj * CW : (jj + 1) * CW] = mg[jj, src + u]

        @pl.loop(0, COLS // 256)
        def _(nt):
            at = pl.ds(pl.multiple_of(nt * 256, 256), 256)
            prod = jnp.dot(fg[j], mgp[:, at], preferred_element_type=F32)
            if j == 0:
                acc[:, at] = prod
            else:
                acc[:, at] += prod

    def iterate_chunk(j):
        own = mg[j, pl.ds(r * UNITS, UNITS)].reshape(ROWS, CW).astype(F32)
        value = 0.5 * (3.0 * own - acc[:, j * CW : (j + 1) * CW])
        for a in range(8):
            rows = slice(a * BW, (a + 1) * BW)
            acc[rows, j * CW : (j + 1) * CW] = (
                value[rows] * mit[a : a + 1, j * CW : (j + 1) * CW]
            )
        turn_store(1, j, acc[:, j * CW : (j + 1) * CW])

    @pl.loop(0, NB // 2)
    def _(i):
        at = pl.ds(pl.multiple_of(i * 128, 128), 128)
        pltpu.make_async_copy(m_hbm.at[:, at], mine.at[i], m_sem).start()

    barrier = pltpu.get_barrier_semaphore()
    for d in range(1, NR):
        t = lax.rem(r + d, NR)
        pl.semaphore_signal(barrier, inc=1, device_id=(t, group_col(t)), device_id_type=MESH)
    for d in range(1, NC):
        pl.semaphore_signal(
            barrier, inc=1, device_id=(r, lax.rem(c + d, NC)), device_id_type=MESH
        )
    odd[...] = columns_of((lax.broadcasted_iota(jnp.int32, (8, NB), 1) % 2).astype(F32))
    pltpu.make_async_copy(mine, mine, m_sem).wait()
    columns(0)
    pl.semaphore_wait(barrier, NR + NC - 2)

    def own_send(j):
        outer_send(j, 0)
        for p in range(3):
            sib_copy(j, p, 0).start()

    own_send(0)
    for j in range(1, NCH):
        columns(j)
    filters()
    for a in range(NCH + 1):
        if a < NCH:
            outer_wait(a, 0)
            outer_send(a, 1)
        if 0 <= a - 2:
            inner_wait(a - 2, 0)
            inner_send(a - 2, 1)
        if a < NCH:
            outer_wait(a, 1)
            outer_send(a, 2)
            if a + 1 < NCH:
                own_send(a + 1)
        if 0 <= a - 2:
            inner_wait(a - 2, 1)
            inner_send(a - 2, 2)
        if 0 <= a - 1:
            outer_wait(a - 1, 2)
            sib_wait(a - 1)
            first_product(a - 1)
            inner_send(a - 1, 0)
            turn_store(0, a - 1, facc[...])

    last = NCH - 1
    for u in range(U):
        turn1_send(0, u)
    for j in range(last):
        inner_wait(j, 2)
    second_product(0)
    inner_wait(last, 0)
    inner_send(last, 1)
    second_product(1)
    inner_wait(last, 1)
    inner_send(last, 2)
    for j in range(2, last):
        second_product(j)
    for u in range(U):
        turn_on(0, u)
    inner_wait(last, 2)
    second_product(last)
    for j in range(NCH):
        iterate_chunk(j)
    for u in range(U):
        turn1_send(1, u)
    for u in range(U):
        turn_on(1, u)
    for w in range(2):
        for u in range(U):
            turn_end(w, u)

    for j in range(NCH):
        for o in range(3):
            for p, sub, d in stage(o):
                outer_copy(j, p, sub | (1 << d), d, sub).wait_send()
                inner_copy(j, p, sub | (1 << d), d, sub).wait_send()
        for p in range(3):
            for mask in range(8):
                sib_copy(j, p, mask).wait_send()
    for w in range(2):
        for u in range(U):
            for d in range(1, NR):
                turn1(w, u, lax.rem(r + d, NR), r).wait_send()
            for d in range(1, NC):
                turn2(w, u, lax.rem(c + d, NC), lab).wait_send()


def per_device(matrix, position, square_pattern, iterate_pattern):
    numbers = jnp.arange(NB, dtype=jnp.int32)
    inverse = jnp.sum(jnp.where(position[:, None] == numbers[None, :], numbers[:, None], 0), axis=0)
    vmem = pl.BlockSpec(memory_space=pltpu.VMEM)
    smem = pl.BlockSpec(memory_space=pltpu.SMEM)
    dma = pltpu.SemaphoreType.DMA
    return pl.pallas_call(
        kernel,
        out_shape=[jax.ShapeDtypeStruct((ROWS, COLS), BF)] * 2,
        in_specs=[smem, smem, pl.BlockSpec(memory_space=pl.ANY), vmem, vmem, vmem],
        out_specs=[vmem, vmem],
        scratch_shapes=[
            pltpu.VMEM((NB // 2, ROWS, 2 * BW), BF),
            pltpu.VMEM((NCH, M // SUB, SUB, CW), BF),
            pltpu.VMEM((NCH, ROWS, KT), BF),
            pltpu.VMEM((ROWS, CW), F32),
            pltpu.VMEM((KT, COLS), BF),
            pltpu.VMEM((ROWS, COLS), F32),
            pltpu.VMEM((2, U, NR, 4, UR, 128), BF),
            pltpu.VMEM((2, U, NC, UR, COLS), BF),
            pltpu.VMEM((8, COLS), F32),
            pltpu.VMEM((8, COLS), F32),
            pltpu.VMEM((8, COLS), F32),
            pltpu.VMEM((NB // 2, 128), F32),
            dma((NCH, 3, 7)), dma((NCH, 3, 7)),
            dma((NCH, 3, 8)), dma((NCH, 3, 8)),
            dma((NCH, 3, 7)), dma((NCH, 3, 7)),
            dma((2, U, NR)), dma((2, U, NR)),
            dma((2, U, NC)), dma((2, U, NC)),
            dma((2, 2, U)),
            dma,
            *[pltpu.VMEM((NB // 2, UR, 128), BF)] * (2 * U),
        ],
        compiler_params=pltpu.CompilerParams(
            collective_id=0, has_side_effects=True, vmem_limit_bytes=60 << 20
        ),
        cost_estimate=pl.CostEstimate(
            flops=4 * ROWS * M * COLS, bytes_accessed=12 << 20, transcendentals=0
        ),
        name="sign_step",
    )(
        inverse * (BW // SUB), inverse // 2, matrix, position.reshape(1, NB),
        square_pattern, iterate_pattern,
    )


def solution(mesh):
    return jax.shard_map(
        per_device,
        mesh=mesh,
        in_specs=(P("row", None), P(), P(), P()),
        out_specs=(P("row", "col"), P("row", "col")),
        check_vma=False,
    )
```

```python
import jax
import jax.numpy as jnp
from jax import lax
from jax.experimental import pallas as pl
from jax.experimental.pallas import tpu as pltpu
from jax.sharding import PartitionSpec as P

BW = 64
M = 8192
NB = M // BW
ROWS = 512
NR = 16
NC = 8
COLS = M // NC
TW = 128
NT = COLS // TW
CHUNKS = ((0, 1), (1, 1), (2, 1), (3, 1), (4, 1), (5, 1), (6, 1), (7, 1))
PRODUCTS = ((0, 2), (2, 2), (4, 2), (6, 1), (7, 1))
NCH = len(CHUNKS)
WAVES = ((1, 2, 4), (3, 6, 5), (7,))
SUB = 16
UNITS = ROWS // SUB
PARTS = ((0, 11), (11, 11), (22, 10))
U = 2
UR = BW // U
MESH = pl.DeviceIdType.MESH
OUT, SIB, MUL, IN, TURN, MUL2 = range(6)
ORDER = (
    (OUT, 0, 0), (OUT, 0, 1), (OUT, 1, 0), (SIB, 0, 0), (MUL, 0, 0), (OUT, 1, 1),
    (SIB, 0, 1), (OUT, 2, 0), (SIB, 1, 0), (MUL, 0, 1), (OUT, 0, 2), (SIB, 2, 0),
    (MUL, 1, 0), (OUT, 2, 1), (SIB, 1, 1), (MUL, 2, 0), (IN, 0, 0), (OUT, 0, 3),
    (MUL, 1, 1), (OUT, 1, 2), (SIB, 2, 1), (SIB, 0, 2), (MUL, 2, 1), (IN, 1, 0),
    (IN, 0, 1), (OUT, 1, 3), (SIB, 0, 3), (MUL, 0, 2), (OUT, 2, 2), (SIB, 1, 2),
    (MUL, 0, 3), (OUT, 0, 4), (MUL, 1, 2), (OUT, 2, 3), (SIB, 2, 2), (SIB, 1, 3),
    (IN, 2, 0), (IN, 1, 1), (OUT, 0, 5), (MUL, 2, 2), (IN, 0, 2), (SIB, 2, 3),
    (MUL, 1, 3), (OUT, 1, 4), (SIB, 0, 4), (MUL, 2, 3), (OUT, 1, 5), (IN, 2, 1),
    (IN, 0, 3), (SIB, 0, 5), (MUL, 0, 4), (IN, 1, 2), (OUT, 0, 6), (MUL, 0, 5),
    (OUT, 2, 4), (SIB, 1, 4), (OUT, 2, 5), (SIB, 1, 5), (IN, 1, 3), (MUL, 1, 4),
    (IN, 2, 2), (OUT, 0, 7), (SIB, 2, 4), (MUL, 1, 5), (OUT, 1, 6), (SIB, 2, 5),
    (SIB, 0, 6), (MUL, 2, 4), (IN, 2, 3), (IN, 0, 4), (MUL, 2, 5), (IN, 0, 5),
    (MUL, 0, 6), (OUT, 2, 6), (OUT, 1, 7), (SIB, 1, 6), (SIB, 0, 7), (MUL, 1, 6),
    (IN, 1, 4), (IN, 1, 5), (SIB, 2, 6), (MUL, 0, 7), (OUT, 2, 7), (SIB, 1, 7),
    (MUL, 2, 6), (IN, 0, 6), (MUL, 1, 7), (SIB, 2, 7), (IN, 2, 4), (MUL, 2, 7),
    (IN, 2, 5), (IN, 0, 7), (TURN, 0, 0), (IN, 1, 6), (MUL2, 0, 0), (IN, 1, 7),
    (MUL2, 0, 1), (IN, 2, 6), (MUL2, 0, 2), (IN, 2, 7), (MUL2, 0, 3), (MUL2, 0, 4),
)
BF = jnp.bfloat16
F32 = jnp.float32


def flip(v, b):
    return v + b - 2 * v * b


def message(wave, d):
    held = (0, 1 << (d + 2) % 3, 7 - (1 << d))[wave]
    return held, held | (1 << d)


def kernel(
    first, pair, m_hbm, pos_row, sq_pat, it_pat,
    sq_ref, it_ref,
    mine, mg, fg, facc, acc, turned, spread, msq, mit, odd, odd_all,
    xs, xr, ds, dr, ns, nr, t1s, t1r, t2s, t2r, loc, m_sem, *got,
):
    r = lax.axis_index("row")
    c = lax.axis_index("col")
    k = r % 2
    y = (r // 2) % 4
    zh = r // 8
    x = c // 2
    zl = c % 2
    jz = flip(zl, zh)
    lab = x * 2 + jz

    def group_col(row):
        return x * 2 + flip(jz, row // 8)

    def outer(mask):
        y_ = y
        if mask & 1:
            y_ = y_ + 1 - 2 * (y_ % 2)
        if mask & 2:
            y_ = 3 - y_
        zh_ = 1 - zh if mask & 4 else zh
        return (zh_ * 4 + y_) * 2 + k

    def inner(mask):
        x_ = x
        if mask & 1:
            x_ = x_ + 1 - 2 * (x_ % 2)
        if mask & 2:
            x_ = 3 - x_
        zl_ = 1 - zl if mask & 4 else zl
        return x_ * 2 + zl_

    def label(col):
        return col // 2 * 2 + flip(col % 2, zh)

    outer_dev = [(outer(1 << d), group_col(outer(1 << d))) for d in range(3)]
    inner_dev = [(r, inner(1 << d)) for d in range(3)]
    sibling = (r + 1 - 2 * k, c)

    def outer_copy(j, wave, d, theirs=False):
        lo, n = PARTS[d] if wave == 2 else (0, UNITS)
        at = mg.at[pl.ds(*CHUNKS[j]), pl.ds(outer(message(wave, d)[theirs]) * UNITS + lo, n)]
        return pltpu.make_async_remote_copy(
            src_ref=at, dst_ref=at, send_sem=xs.at[j, wave, d], recv_sem=xr.at[j, wave, d],
            device_id=outer_dev[d], device_id_type=MESH,
        )

    def inner_copy(j, wave, d, theirs=False):
        lo, n = PARTS[d] if wave == 2 else (0, UNITS)
        at = fg.at[
            pl.ds(*CHUNKS[j]), label(inner(message(wave, d)[theirs])), pl.ds(lo * SUB, n * SUB)
        ]
        return pltpu.make_async_remote_copy(
            src_ref=at, dst_ref=at, send_sem=ns.at[j, wave, d], recv_sem=nr.at[j, wave, d],
            device_id=inner_dev[d], device_id_type=MESH,
        )

    def sib_copy(j, mask, theirs=False):
        row = outer(mask)
        if theirs:
            row = row + 1 - 2 * k
        at = mg.at[pl.ds(*CHUNKS[j]), pl.ds(row * UNITS, UNITS)]
        return pltpu.make_async_remote_copy(
            src_ref=at, dst_ref=at, send_sem=ds.at[j, mask], recv_sem=dr.at[j, mask],
            device_id=sibling, device_id_type=MESH,
        )

    def outer_send(j, wave):
        for d in range(3):
            outer_copy(j, wave, d).start()

    def outer_wait(j, wave):
        for d in range(3):
            outer_copy(j, wave, d, theirs=True).wait_recv()

    def sib_send(j, wave):
        for mask in WAVES[wave]:
            sib_copy(j, mask).start()

    def inner_send(j, wave):
        for d in range(3):
            inner_copy(j, wave, d).start()

    def inner_wait(j, wave):
        for d in range(3):
            inner_copy(j, wave, d, theirs=True).wait_recv()

    def sib_wait(j, masks):
        for mask in masks:
            sib_copy(j, mask, theirs=True).wait_recv()

    def turn1(w, u, t, src_row):
        return pltpu.make_async_remote_copy(
            src_ref=turned.at[w, u, t], dst_ref=got[w * U + u].at[pl.ds(4 * src_row, 4)],
            send_sem=t1s.at[w, u, t], recv_sem=t1r.at[w, u, src_row],
            device_id=(t, group_col(t)), device_id_type=MESH,
        )

    def turn1_own(w, u):
        return pltpu.make_async_copy(
            turned.at[w, u, r], got[w * U + u].at[pl.ds(4 * r, 4)], loc.at[0, w, u]
        )

    def turn2(w, u, col, src_lab):
        out = (sq_ref, it_ref)[w]
        return pltpu.make_async_remote_copy(
            src_ref=spread.at[w, u, col],
            dst_ref=out.at[pl.ds(pl.multiple_of(src_lab * BW + u * UR, UR), UR)],
            send_sem=t2s.at[w, u, col], recv_sem=t2r.at[w, u, src_lab],
            device_id=(r, col), device_id_type=MESH,
        )

    def turn2_own(w, u):
        out = (sq_ref, it_ref)[w]
        return pltpu.make_async_copy(
            spread.at[w, u, c],
            out.at[pl.ds(pl.multiple_of(lab * BW + u * UR, UR), UR)],
            loc.at[1, w, u],
        )

    def turn_store(w, tile, tiles, values):
        flat = values.T.astype(BF)
        for i in range(2 * tiles):
            for u in range(U):
                for n in range(4):
                    lo = i * BW + u * UR
                    turned[w, u, 2 * tile + i, n] = flat[lo : lo + UR, n * 128 : (n + 1) * 128]

    def turn1_send(w, u):
        for d in range(1, NR):
            turn1(w, u, lax.rem(r + d, NR), r).start()
        turn1_own(w, u).start()

    def turn_on(w, u):
        for d in range(1, NR):
            t = lax.rem(r + NR - d, NR)
            turn1(w, u, t, t).wait_recv()
        turn1_own(w, u).wait()
        have = got[w * U + u]
        lane = lax.broadcasted_iota(jnp.int32, (UR, 128), 1)
        for col in range(NC):
            for g in range(8):
                q = 16 * col + 2 * g
                w0 = have[pair[q]].astype(F32)
                w1 = have[pair[q + 1]].astype(F32)
                o = odd_all[q // 2 : q // 2 + 1, :]
                lo = w0 * (1.0 - o) + pltpu.roll(w0, BW, 1) * o
                hi = w1 * o + pltpu.roll(w1, BW, 1) * (1.0 - o)
                spread[w, u, col, :, g * 128 : (g + 1) * 128] = jnp.where(
                    lane < BW, lo, hi
                ).astype(BF)
        for d in range(1, NC):
            turn2(w, u, lax.rem(c + d, NC), lab).start()
        turn2_own(w, u).start()

    def turn_end(w, u):
        for d in range(1, NC):
            col = lax.rem(c + NC - d, NC)
            turn2(w, u, col, label(col)).wait_recv()
        turn2_own(w, u).wait()

    def columns(j):
        lane = lax.broadcasted_iota(jnp.int32, (ROWS, TW), 1)
        tile, tiles = CHUNKS[j]
        for i in range(tile, tile + tiles):
            w0 = mine[pair[8 * (2 * i) + lab]].astype(F32)
            w1 = mine[pair[8 * (2 * i + 1) + lab]].astype(F32)
            o = odd[0:1, i * TW : (i + 1) * TW]
            lo = w0 * (1.0 - o) + pltpu.roll(w0, BW, 1) * o
            hi = w1 * o + pltpu.roll(w1, BW, 1) * (1.0 - o)
            both = jnp.where(lane < BW, lo, hi).astype(BF).reshape(UNITS, SUB, TW)
            mg[i, pl.ds(r * UNITS, UNITS)] = both

    def columns_of(rows):
        block_id = lax.broadcasted_iota(jnp.int32, (NR, NB), 0)
        hot = (pos_row[...] == 8 * block_id + lab).astype(F32)
        wide = (
            lax.broadcasted_iota(jnp.int32, (NR, COLS), 1) // BW
            == lax.broadcasted_iota(jnp.int32, (NR, COLS), 0)
        ).astype(F32)
        small = lax.dot_general(rows, hot, (((1,), (1,)), ((), ())), preferred_element_type=F32)
        return jnp.dot(small, wide, preferred_element_type=F32)

    def filters():
        at = pl.ds(pl.multiple_of(8 * r, 8), 8)
        msq[...] = columns_of(sq_pat[at, :].astype(F32))
        mit[...] = columns_of(it_pat[at, :].astype(F32))
        parity = (lax.broadcasted_iota(jnp.int32, (NB, NB), 0) % 2).astype(F32)
        half = lax.broadcasted_iota(jnp.int32, (NB // 2, NB), 0)
        evens = (pos_row[...] == 2 * half).astype(F32)
        odds = (pos_row[...] == 2 * half + 1).astype(F32)
        lane = lax.broadcasted_iota(jnp.int32, (NB // 2, NB), 1)
        odd_all[...] = jnp.where(
            lane < BW,
            jnp.dot(evens, parity, preferred_element_type=F32),
            jnp.dot(odds, parity, preferred_element_type=F32),
        )

    def first_product(j, masks):
        tile, tiles = CHUNKS[j]
        total = facc.at[j % 2, :, 0 : tiles * TW]
        for mask in masks:
            chip = outer(mask) // 2
            left = jnp.concatenate([mine[chip * 8 + i] for i in range(8)], axis=1)
            right = jnp.concatenate(
                [
                    mg[i, pl.ds(chip * 64, 64)].reshape(1024, TW)
                    for i in range(tile, tile + tiles)
                ],
                axis=1,
            )
            prod = jnp.dot(left, right, preferred_element_type=F32)
            if mask == 0:
                total[...] = prod
            else:
                total[...] += prod

    def first_filter(j):
        tile, tiles = CHUNKS[j]
        for a in range(8):
            rows = slice(a * BW, (a + 1) * BW)
            for i in range(tiles):
                at = slice(i * TW, (i + 1) * TW)
                of = slice((tile + i) * TW, (tile + i + 1) * TW)
                value = facc[j % 2, rows, at] * msq[a : a + 1, of]
                facc[j % 2, rows, at] = value
                fg[tile + i, lab, rows, :] = value.astype(BF)

    def second_product(i):
        tile, tiles = PRODUCTS[i]

        @pl.loop(0, COLS // 256)
        def _(nt):
            at = pl.ds(pl.multiple_of(nt * 256, 256), 256)
            left = jnp.concatenate(
                [fg[t, n] for t in range(tile, tile + tiles) for n in range(NC)], axis=1
            )
            right = jnp.concatenate(
                [
                    jnp.concatenate(
                        [mg[nt * 2 + h, first[8 * (2 * t + b) + n] + u] for h in range(2)], axis=1
                    )
                    for t in range(tile, tile + tiles)
                    for n in range(NC)
                    for b in range(2)
                    for u in range(BW // SUB)
                ],
                axis=0,
            )
            prod = jnp.dot(left, right, preferred_element_type=F32)
            if tile == 0:
                acc[:, at] = prod
            else:
                acc[:, at] += prod

    def iterate_tiles(tile):
        own = jnp.concatenate(
            [mg[tile + i, pl.ds(r * UNITS, UNITS)].reshape(ROWS, TW) for i in range(2)], axis=1
        )
        at = slice(tile * TW, (tile + 2) * TW)
        value = 0.5 * (3.0 * own.astype(F32) - acc[:, at])
        kept = [value[a * BW : (a + 1) * BW] * mit[a : a + 1, at] for a in range(8)]
        turn_store(1, tile, 2, jnp.concatenate(kept, axis=0))

    @pl.loop(0, NB // 2)
    def _(i):
        at = pl.ds(pl.multiple_of(i * 128, 128), 128)
        pltpu.make_async_copy(m_hbm.at[:, at], mine.at[i], m_sem).start()

    barrier = pltpu.get_barrier_semaphore()
    for d in range(1, NR):
        t = lax.rem(r + d, NR)
        pl.semaphore_signal(barrier, inc=1, device_id=(t, group_col(t)), device_id_type=MESH)
    for d in range(1, NC):
        pl.semaphore_signal(
            barrier, inc=1, device_id=(r, lax.rem(c + d, NC)), device_id_type=MESH
        )
    odd[...] = columns_of((lax.broadcasted_iota(jnp.int32, (8, NB), 1) % 2).astype(F32))
    pltpu.make_async_copy(mine, mine, m_sem).wait()
    columns(0)
    pl.semaphore_wait(barrier, NR + NC - 2)

    def own_send(j):
        outer_send(j, 0)
        sib_copy(j, 0).start()

    seen = set()

    def once(f, *args):
        if (f, *args) not in seen:
            seen.add((f, *args))
            f(*args)

    for step, wave, j in ORDER:
        if step == OUT:
            if wave == 0:
                once(columns, j)
                own_send(j)
            else:
                once(outer_wait, j, wave - 1)
                outer_send(j, wave)
            if j == 1 and wave == 0:
                for i in range(2, NCH):
                    once(columns, i)
                filters()
        elif step == SIB:
            once(outer_wait, j, wave)
            sib_send(j, wave)
        elif step == MUL:
            masks = ((0, 1, 2, 4), (3, 6, 5), (7,))[wave]
            sib_wait(j, masks)
            first_product(j, masks)
            if wave == 2:
                first_filter(j)
        elif step == IN:
            if wave == 0:
                inner_send(j, 0)
                tile, tiles = CHUNKS[j]
                turn_store(0, tile, tiles, facc[j % 2, :, 0 : tiles * TW])
            else:
                once(inner_wait, j, wave - 1)
                inner_send(j, wave)
        elif step == TURN:
            for u in range(U):
                turn1_send(0, u)
        else:
            for i in range(NCH):
                if CHUNKS[i][0] < sum(PRODUCTS[j]):
                    once(inner_wait, i, 2)
            second_product(j)

    for tile in range(0, NT, 2):
        iterate_tiles(tile)
    for u in range(U):
        turn1_send(1, u)
    for u in range(U):
        turn_on(0, u)
    for u in range(U):
        turn_on(1, u)
    for w in range(2):
        for u in range(U):
            turn_end(w, u)

    for j in range(NCH):
        for wave in range(3):
            for d in range(3):
                outer_copy(j, wave, d).wait_send()
                inner_copy(j, wave, d).wait_send()
        for mask in range(8):
            sib_copy(j, mask).wait_send()
    for w in range(2):
        for u in range(U):
            for d in range(1, NR):
                turn1(w, u, lax.rem(r + d, NR), r).wait_send()
            for d in range(1, NC):
                turn2(w, u, lax.rem(c + d, NC), lab).wait_send()


def per_device(matrix, position, square_pattern, iterate_pattern):
    numbers = jnp.arange(NB, dtype=jnp.int32)
    inverse = jnp.sum(jnp.where(position[:, None] == numbers[None, :], numbers[:, None], 0), axis=0)
    vmem = pl.BlockSpec(memory_space=pltpu.VMEM)
    smem = pl.BlockSpec(memory_space=pltpu.SMEM)
    dma = pltpu.SemaphoreType.DMA
    return pl.pallas_call(
        kernel,
        out_shape=[jax.ShapeDtypeStruct((ROWS, COLS), BF)] * 2,
        in_specs=[smem, smem, pl.BlockSpec(memory_space=pl.ANY), vmem, vmem, vmem],
        out_specs=[vmem, vmem],
        scratch_shapes=[
            pltpu.VMEM((NB // 2, ROWS, 2 * BW), BF),
            pltpu.VMEM((NT, M // SUB, SUB, TW), BF),
            pltpu.VMEM((NT, NC, ROWS, TW), BF),
            pltpu.VMEM((2, ROWS, 2 * TW), F32),
            pltpu.VMEM((ROWS, COLS), F32),
            pltpu.VMEM((2, U, NR, 4, UR, 128), BF),
            pltpu.VMEM((2, U, NC, UR, COLS), BF),
            pltpu.VMEM((8, COLS), F32),
            pltpu.VMEM((8, COLS), F32),
            pltpu.VMEM((8, COLS), F32),
            pltpu.VMEM((NB // 2, 128), F32),
            dma((NCH, 3, 3)), dma((NCH, 3, 3)),
            dma((NCH, NC)), dma((NCH, NC)),
            dma((NCH, 3, 3)), dma((NCH, 3, 3)),
            dma((2, U, NR)), dma((2, U, NR)),
            dma((2, U, NC)), dma((2, U, NC)),
            dma((2, 2, U)),
            dma,
            *[pltpu.VMEM((NB // 2, UR, 128), BF)] * (2 * U),
        ],
        compiler_params=pltpu.CompilerParams(
            collective_id=0, has_side_effects=True, vmem_limit_bytes=60 << 20
        ),
        cost_estimate=pl.CostEstimate(
            flops=4 * ROWS * M * COLS, bytes_accessed=12 << 20, transcendentals=0
        ),
        name="sign_step",
    )(
        inverse * (BW // SUB), inverse // 2, matrix, position.reshape(1, NB),
        square_pattern, iterate_pattern,
    )


def solution(mesh):
    return jax.shard_map(
        per_device,
        mesh=mesh,
        in_specs=(P("row", None), P(), P(), P()),
        out_specs=(P("row", "col"), P("row", "col")),
        check_vma=False,
    )
```

```python
import jax
import jax.numpy as jnp
from jax import lax
from jax.experimental import pallas as pl
from jax.experimental.pallas import tpu as pltpu
from jax.sharding import PartitionSpec as P

BW = 64
M = 8192
NB = M // BW
ROWS = 512
NR = 16
NC = 8
COLS = M // NC
TW = 128
NT = COLS // TW
CHUNKS = ((0, 1), (1, 1), (2, 1), (3, 1), (4, 1), (5, 1), (6, 1), (7, 1))
PRODUCTS = ((0, 2), (2, 2), (4, 2), (6, 1), (7, 1))
NCH = len(CHUNKS)
WAVES = ((1, 2, 4), (3, 6, 5), (7,))
SUB = 16
UNITS = ROWS // SUB
PARTS = ((0, 11), (11, 11), (22, 10))
U = 2
UR = BW // U
MESH = pl.DeviceIdType.MESH
OUT, SIB, MUL, IN, TURN, MUL2 = range(6)
ORDER = (
    (OUT, 0, 0), (OUT, 0, 1), (OUT, 1, 0), (SIB, 0, 0), (OUT, 1, 1), (SIB, 0, 1),
    (MUL, 0, 0), (OUT, 2, 0), (OUT, 0, 2), (SIB, 1, 0), (MUL, 0, 1), (OUT, 2, 1),
    (SIB, 1, 1), (MUL, 1, 0), (OUT, 0, 3), (SIB, 2, 0), (MUL, 1, 1), (OUT, 1, 2),
    (SIB, 2, 1), (SIB, 0, 2), (MUL, 2, 0), (IN, 0, 0), (OUT, 0, 4), (OUT, 1, 3),
    (SIB, 0, 3), (MUL, 2, 1), (IN, 0, 1), (OUT, 2, 2), (SIB, 1, 2), (MUL, 0, 2),
    (IN, 1, 0), (OUT, 0, 5), (MUL, 1, 2), (IN, 1, 1), (SIB, 2, 2), (MUL, 0, 3),
    (OUT, 2, 3), (OUT, 1, 4), (SIB, 1, 3), (IN, 2, 0), (SIB, 0, 4), (OUT, 1, 5),
    (SIB, 0, 5), (MUL, 2, 2), (IN, 2, 1), (IN, 0, 2), (SIB, 2, 3), (MUL, 1, 3),
    (OUT, 0, 6), (MUL, 0, 4), (OUT, 2, 4), (OUT, 2, 5), (SIB, 1, 4), (SIB, 1, 5),
    (IN, 1, 2), (OUT, 0, 7), (MUL, 2, 3), (IN, 0, 3), (OUT, 1, 6), (SIB, 0, 6),
    (SIB, 2, 4), (SIB, 2, 5), (MUL, 1, 4), (MUL, 0, 5), (OUT, 1, 7), (IN, 2, 2),
    (IN, 1, 3), (SIB, 0, 7), (OUT, 2, 6), (SIB, 1, 6), (MUL, 2, 4), (IN, 0, 4),
    (MUL, 1, 5), (MUL, 2, 5), (OUT, 2, 7), (IN, 2, 3), (IN, 0, 5), (SIB, 2, 6),
    (SIB, 1, 7), (MUL, 0, 6), (IN, 1, 4), (SIB, 2, 7), (MUL, 1, 6), (MUL, 2, 6),
    (IN, 1, 5), (IN, 0, 6), (MUL, 0, 7), (IN, 2, 4), (MUL, 1, 7), (MUL, 2, 7),
    (IN, 0, 7), (TURN, 0, 0), (IN, 2, 5), (IN, 1, 6), (MUL2, 0, 0), (IN, 1, 7),
    (MUL2, 0, 1), (IN, 2, 6), (MUL2, 0, 2), (IN, 2, 7), (MUL2, 0, 3), (MUL2, 0, 4),
)
BF = jnp.bfloat16
F32 = jnp.float32


def flip(v, b):
    return v + b - 2 * v * b


def message(wave, d):
    held = (0, 1 << (d + 2) % 3, 7 - (1 << d))[wave]
    return held, held | (1 << d)


def kernel(
    first, pair, m_hbm, pos_row, sq_pat, it_pat,
    sq_ref, it_ref,
    mine, mg, fg, facc, acc, turned, spread, msq, mit, odd, odd_all,
    xs, xr, ds, dr, ns, nr, t1s, t1r, t2s, t2r, loc, m_sem, *got,
):
    r = lax.axis_index("row")
    c = lax.axis_index("col")
    k = r % 2
    y = (r // 2) % 4
    zh = r // 8
    x = c // 2
    zl = c % 2
    jz = flip(zl, zh)
    lab = x * 2 + jz

    def group_col(row):
        return x * 2 + flip(jz, row // 8)

    def outer(mask):
        y_ = y
        if mask & 1:
            y_ = y_ + 1 - 2 * (y_ % 2)
        if mask & 2:
            y_ = 3 - y_
        zh_ = 1 - zh if mask & 4 else zh
        return (zh_ * 4 + y_) * 2 + k

    def inner(mask):
        x_ = x
        if mask & 1:
            x_ = x_ + 1 - 2 * (x_ % 2)
        if mask & 2:
            x_ = 3 - x_
        zl_ = 1 - zl if mask & 4 else zl
        return x_ * 2 + zl_

    def label(col):
        return col // 2 * 2 + flip(col % 2, zh)

    outer_dev = [(outer(1 << d), group_col(outer(1 << d))) for d in range(3)]
    inner_dev = [(r, inner(1 << d)) for d in range(3)]
    sibling = (r + 1 - 2 * k, c)

    def outer_copy(j, wave, d, theirs=False):
        lo, n = PARTS[d] if wave == 2 else (0, UNITS)
        at = mg.at[pl.ds(*CHUNKS[j]), pl.ds(outer(message(wave, d)[theirs]) * UNITS + lo, n)]
        return pltpu.make_async_remote_copy(
            src_ref=at, dst_ref=at, send_sem=xs.at[j, wave, d], recv_sem=xr.at[j, wave, d],
            device_id=outer_dev[d], device_id_type=MESH,
        )

    def inner_copy(j, wave, d, theirs=False):
        lo, n = PARTS[d] if wave == 2 else (0, UNITS)
        at = fg.at[
            pl.ds(*CHUNKS[j]), label(inner(message(wave, d)[theirs])), pl.ds(lo * SUB, n * SUB)
        ]
        return pltpu.make_async_remote_copy(
            src_ref=at, dst_ref=at, send_sem=ns.at[j, wave, d], recv_sem=nr.at[j, wave, d],
            device_id=inner_dev[d], device_id_type=MESH,
        )

    def sib_copy(j, mask, theirs=False):
        row = outer(mask)
        if theirs:
            row = row + 1 - 2 * k
        at = mg.at[pl.ds(*CHUNKS[j]), pl.ds(row * UNITS, UNITS)]
        return pltpu.make_async_remote_copy(
            src_ref=at, dst_ref=at, send_sem=ds.at[j, mask], recv_sem=dr.at[j, mask],
            device_id=sibling, device_id_type=MESH,
        )

    def outer_send(j, wave):
        for d in range(3):
            outer_copy(j, wave, d).start()

    def outer_wait(j, wave):
        for d in range(3):
            outer_copy(j, wave, d, theirs=True).wait_recv()

    def sib_send(j, wave):
        for mask in WAVES[wave]:
            sib_copy(j, mask).start()

    def inner_send(j, wave):
        for d in range(3):
            inner_copy(j, wave, d).start()

    def inner_wait(j, wave):
        for d in range(3):
            inner_copy(j, wave, d, theirs=True).wait_recv()

    def sib_wait(j, masks):
        for mask in masks:
            sib_copy(j, mask, theirs=True).wait_recv()

    def turn1(w, u, t, src_row):
        return pltpu.make_async_remote_copy(
            src_ref=turned.at[w, u, t], dst_ref=got[w * U + u].at[pl.ds(4 * src_row, 4)],
            send_sem=t1s.at[w, u, t], recv_sem=t1r.at[w, u, src_row],
            device_id=(t, group_col(t)), device_id_type=MESH,
        )

    def turn1_own(w, u):
        return pltpu.make_async_copy(
            turned.at[w, u, r], got[w * U + u].at[pl.ds(4 * r, 4)], loc.at[0, w, u]
        )

    def turn2(w, u, col, src_lab):
        out = (sq_ref, it_ref)[w]
        return pltpu.make_async_remote_copy(
            src_ref=spread.at[w, u, col],
            dst_ref=out.at[pl.ds(pl.multiple_of(src_lab * BW + u * UR, UR), UR)],
            send_sem=t2s.at[w, u, col], recv_sem=t2r.at[w, u, src_lab],
            device_id=(r, col), device_id_type=MESH,
        )

    def turn2_own(w, u):
        out = (sq_ref, it_ref)[w]
        return pltpu.make_async_copy(
            spread.at[w, u, c],
            out.at[pl.ds(pl.multiple_of(lab * BW + u * UR, UR), UR)],
            loc.at[1, w, u],
        )

    def turn_store(w, tile, tiles, values):
        flat = values.T.astype(BF)
        for i in range(2 * tiles):
            for u in range(U):
                for n in range(4):
                    lo = i * BW + u * UR
                    turned[w, u, 2 * tile + i, n] = flat[lo : lo + UR, n * 128 : (n + 1) * 128]

    def turn1_send(w, u):
        for d in range(1, NR):
            turn1(w, u, lax.rem(r + d, NR), r).start()
        turn1_own(w, u).start()

    def turn_on(w, u):
        for d in range(1, NR):
            t = lax.rem(r + NR - d, NR)
            turn1(w, u, t, t).wait_recv()
        turn1_own(w, u).wait()
        have = got[w * U + u]
        lane = lax.broadcasted_iota(jnp.int32, (UR, 128), 1)
        for col in range(NC):
            for g in range(8):
                q = 16 * col + 2 * g
                w0 = have[pair[q]].astype(F32)
                w1 = have[pair[q + 1]].astype(F32)
                o = odd_all[q // 2 : q // 2 + 1, :]
                lo = w0 * (1.0 - o) + pltpu.roll(w0, BW, 1) * o
                hi = w1 * o + pltpu.roll(w1, BW, 1) * (1.0 - o)
                spread[w, u, col, :, g * 128 : (g + 1) * 128] = jnp.where(
                    lane < BW, lo, hi
                ).astype(BF)
        for d in range(1, NC):
            turn2(w, u, lax.rem(c + d, NC), lab).start()
        turn2_own(w, u).start()

    def turn_end(w, u):
        for d in range(1, NC):
            col = lax.rem(c + NC - d, NC)
            turn2(w, u, col, label(col)).wait_recv()
        turn2_own(w, u).wait()

    def columns(j):
        lane = lax.broadcasted_iota(jnp.int32, (ROWS, TW), 1)
        tile, tiles = CHUNKS[j]
        for i in range(tile, tile + tiles):
            w0 = mine[pair[8 * (2 * i) + lab]].astype(F32)
            w1 = mine[pair[8 * (2 * i + 1) + lab]].astype(F32)
            o = odd[0:1, i * TW : (i + 1) * TW]
            lo = w0 * (1.0 - o) + pltpu.roll(w0, BW, 1) * o
            hi = w1 * o + pltpu.roll(w1, BW, 1) * (1.0 - o)
            both = jnp.where(lane < BW, lo, hi).astype(BF).reshape(UNITS, SUB, TW)
            mg[i, pl.ds(r * UNITS, UNITS)] = both

    def columns_of(rows):
        block_id = lax.broadcasted_iota(jnp.int32, (NR, NB), 0)
        hot = (pos_row[...] == 8 * block_id + lab).astype(F32)
        wide = (
            lax.broadcasted_iota(jnp.int32, (NR, COLS), 1) // BW
            == lax.broadcasted_iota(jnp.int32, (NR, COLS), 0)
        ).astype(F32)
        small = lax.dot_general(rows, hot, (((1,), (1,)), ((), ())), preferred_element_type=F32)
        return jnp.dot(small, wide, preferred_element_type=F32)

    def filters():
        at = pl.ds(pl.multiple_of(8 * r, 8), 8)
        msq[...] = columns_of(sq_pat[at, :].astype(F32))
        mit[...] = columns_of(it_pat[at, :].astype(F32))
        parity = (lax.broadcasted_iota(jnp.int32, (NB, NB), 0) % 2).astype(F32)
        half = lax.broadcasted_iota(jnp.int32, (NB // 2, NB), 0)
        evens = (pos_row[...] == 2 * half).astype(F32)
        odds = (pos_row[...] == 2 * half + 1).astype(F32)
        lane = lax.broadcasted_iota(jnp.int32, (NB // 2, NB), 1)
        odd_all[...] = jnp.where(
            lane < BW,
            jnp.dot(evens, parity, preferred_element_type=F32),
            jnp.dot(odds, parity, preferred_element_type=F32),
        )

    def first_product(j, masks):
        tile, tiles = CHUNKS[j]
        total = facc.at[j % 2, :, 0 : tiles * TW]
        for mask in masks:
            chip = outer(mask) // 2
            left = jnp.concatenate([mine[chip * 8 + i] for i in range(8)], axis=1)
            right = jnp.concatenate(
                [
                    mg[i, pl.ds(chip * 64, 64)].reshape(1024, TW)
                    for i in range(tile, tile + tiles)
                ],
                axis=1,
            )
            prod = jnp.dot(left, right, preferred_element_type=F32)
            if mask == 0:
                total[...] = prod
            else:
                total[...] += prod

    def first_filter(j):
        tile, tiles = CHUNKS[j]
        for a in range(8):
            rows = slice(a * BW, (a + 1) * BW)
            for i in range(tiles):
                at = slice(i * TW, (i + 1) * TW)
                of = slice((tile + i) * TW, (tile + i + 1) * TW)
                value = facc[j % 2, rows, at] * msq[a : a + 1, of]
                facc[j % 2, rows, at] = value
                fg[tile + i, lab, rows, :] = value.astype(BF)

    def second_product(i):
        tile, tiles = PRODUCTS[i]

        @pl.loop(0, COLS // 256)
        def _(nt):
            at = pl.ds(pl.multiple_of(nt * 256, 256), 256)
            left = jnp.concatenate(
                [fg[t, n] for t in range(tile, tile + tiles) for n in range(NC)], axis=1
            )
            right = jnp.concatenate(
                [
                    jnp.concatenate(
                        [mg[nt * 2 + h, first[8 * (2 * t + b) + n] + u] for h in range(2)], axis=1
                    )
                    for t in range(tile, tile + tiles)
                    for n in range(NC)
                    for b in range(2)
                    for u in range(BW // SUB)
                ],
                axis=0,
            )
            prod = jnp.dot(left, right, preferred_element_type=F32)
            if tile == 0:
                acc[:, at] = prod
            else:
                acc[:, at] += prod

    def iterate_tiles(tile):
        own = jnp.concatenate(
            [mg[tile + i, pl.ds(r * UNITS, UNITS)].reshape(ROWS, TW) for i in range(2)], axis=1
        )
        at = slice(tile * TW, (tile + 2) * TW)
        value = 0.5 * (3.0 * own.astype(F32) - acc[:, at])
        kept = [value[a * BW : (a + 1) * BW] * mit[a : a + 1, at] for a in range(8)]
        turn_store(1, tile, 2, jnp.concatenate(kept, axis=0))

    @pl.loop(0, NB // 2)
    def _(i):
        at = pl.ds(pl.multiple_of(i * 128, 128), 128)
        pltpu.make_async_copy(m_hbm.at[:, at], mine.at[i], m_sem).start()

    barrier = pltpu.get_barrier_semaphore()
    for d in range(1, NR):
        t = lax.rem(r + d, NR)
        pl.semaphore_signal(barrier, inc=1, device_id=(t, group_col(t)), device_id_type=MESH)
    for d in range(1, NC):
        pl.semaphore_signal(
            barrier, inc=1, device_id=(r, lax.rem(c + d, NC)), device_id_type=MESH
        )
    odd[...] = columns_of((lax.broadcasted_iota(jnp.int32, (8, NB), 1) % 2).astype(F32))
    pltpu.make_async_copy(mine, mine, m_sem).wait()
    columns(0)
    pl.semaphore_wait(barrier, NR + NC - 2)

    def own_send(j):
        outer_send(j, 0)
        sib_copy(j, 0).start()

    seen = set()

    def once(f, *args):
        if (f, *args) not in seen:
            seen.add((f, *args))
            f(*args)

    for step, wave, j in ORDER:
        if step == OUT:
            if wave == 0:
                once(columns, j)
                own_send(j)
            else:
                once(outer_wait, j, wave - 1)
                outer_send(j, wave)
            if j == 1 and wave == 0:
                for i in range(2, NCH):
                    once(columns, i)
                filters()
        elif step == SIB:
            once(outer_wait, j, wave)
            sib_send(j, wave)
        elif step == MUL:
            masks = ((0, 1, 2, 4), (3, 6, 5), (7,))[wave]
            sib_wait(j, masks)
            first_product(j, masks)
            if wave == 2:
                first_filter(j)
        elif step == IN:
            if wave == 0:
                inner_send(j, 0)
                tile, tiles = CHUNKS[j]
                turn_store(0, tile, tiles, facc[j % 2, :, 0 : tiles * TW])
            else:
                once(inner_wait, j, wave - 1)
                inner_send(j, wave)
        elif step == TURN:
            for u in range(U):
                turn1_send(0, u)
        else:
            for i in range(NCH):
                if CHUNKS[i][0] < sum(PRODUCTS[j]):
                    once(inner_wait, i, 2)
            second_product(j)

    for tile in range(0, NT, 2):
        iterate_tiles(tile)
    for u in range(U):
        turn1_send(1, u)
    for u in range(U):
        turn_on(0, u)
    for u in range(U):
        turn_on(1, u)
    for w in range(2):
        for u in range(U):
            turn_end(w, u)

    for j in range(NCH):
        for wave in range(3):
            for d in range(3):
                outer_copy(j, wave, d).wait_send()
                inner_copy(j, wave, d).wait_send()
        for mask in range(8):
            sib_copy(j, mask).wait_send()
    for w in range(2):
        for u in range(U):
            for d in range(1, NR):
                turn1(w, u, lax.rem(r + d, NR), r).wait_send()
            for d in range(1, NC):
                turn2(w, u, lax.rem(c + d, NC), lab).wait_send()


def hand_over(sq_in, it_in, sq_out, it_out):
    sq_out[...] = sq_in[...]
    it_out[...] = it_in[...]


def per_device(matrix, position, square_pattern, iterate_pattern):
    numbers = jnp.arange(NB, dtype=jnp.int32)
    inverse = jnp.sum(jnp.where(position[:, None] == numbers[None, :], numbers[:, None], 0), axis=0)
    vmem = pl.BlockSpec(memory_space=pltpu.VMEM)
    smem = pl.BlockSpec(memory_space=pltpu.SMEM)
    dma = pltpu.SemaphoreType.DMA
    results = pl.pallas_call(
        kernel,
        out_shape=[jax.ShapeDtypeStruct((ROWS, COLS), BF)] * 2,
        in_specs=[smem, smem, pl.BlockSpec(memory_space=pl.ANY), vmem, vmem, vmem],
        out_specs=[vmem, vmem],
        scratch_shapes=[
            pltpu.VMEM((NB // 2, ROWS, 2 * BW), BF),
            pltpu.VMEM((NT, M // SUB, SUB, TW), BF),
            pltpu.VMEM((NT, NC, ROWS, TW), BF),
            pltpu.VMEM((2, ROWS, 2 * TW), F32),
            pltpu.VMEM((ROWS, COLS), F32),
            pltpu.VMEM((2, U, NR, 4, UR, 128), BF),
            pltpu.VMEM((2, U, NC, UR, COLS), BF),
            pltpu.VMEM((8, COLS), F32),
            pltpu.VMEM((8, COLS), F32),
            pltpu.VMEM((8, COLS), F32),
            pltpu.VMEM((NB // 2, 128), F32),
            dma((NCH, 3, 3)), dma((NCH, 3, 3)),
            dma((NCH, NC)), dma((NCH, NC)),
            dma((NCH, 3, 3)), dma((NCH, 3, 3)),
            dma((2, U, NR)), dma((2, U, NR)),
            dma((2, U, NC)), dma((2, U, NC)),
            dma((2, 2, U)),
            dma,
            *[pltpu.VMEM((NB // 2, UR, 128), BF)] * (2 * U),
        ],
        compiler_params=pltpu.CompilerParams(
            collective_id=0, has_side_effects=True, vmem_limit_bytes=60 << 20
        ),
        cost_estimate=pl.CostEstimate(
            flops=4 * ROWS * M * COLS, bytes_accessed=12 << 20, transcendentals=0
        ),
        name="sign_step",
    )(
        inverse * (BW // SUB), inverse // 2, matrix, position.reshape(1, NB),
        square_pattern, iterate_pattern,
    )
    return pl.pallas_call(
        hand_over,
        out_shape=[jax.ShapeDtypeStruct((ROWS, COLS), BF)] * 2,
        in_specs=[vmem, vmem],
        out_specs=[vmem, vmem],
        name="hand_over",
    )(*results)


def solution(mesh):
    return jax.shard_map(
        per_device,
        mesh=mesh,
        in_specs=(P("row", None), P(), P(), P()),
        out_specs=(P("row", "col"), P("row", "col")),
        check_vma=False,
    )
```
